32 devices in a mesh: groups: 2 (over y), length: 4 (over z), sector: 2 (over x), pair: 2 (over core).
Axes of the slice: x: 2, y: 2, z: 4, core: 2. Of those that a mesh axis runs over, the one named last changes fastest.
Arguments:
- flag_kernels: bfloat16 [4, 8, 32, 25, 1024], P('length', ('groups', 'sector', 'pair')), parts along dimension 1, may hold values from -1.1953125 to 1.1953125
- flag_unary: bfloat16 [4, 8, 32, 8, 1024], P('length', ('groups', 'sector', 'pair')), parts along dimension 1, may hold values from -8 to 8
- flag_labels: int32 [4, 8, 32, 1024], P('length', ('groups', 'sector', 'pair')), parts along dimension 1, may hold values from 0 to 7
- flag_mask: int32 [4, 8, 32, 1024], P('length', ('groups', 'sector', 'pair')), parts along dimension 1, may hold values 0 or 1
- dest_list: int32 [4, 8, 32], P('length', ('groups', 'sector', 'pair')), parts along dimension 1, may hold values from -1 to 3, as said below
- slot_list: int32 [4, 8, 32], P('length', ('groups', 'sector', 'pair')), parts along dimension 1, may hold values from -1 to 15, as said below
- res_kernels: bfloat16 [4, 8, 8, 25, 1024], P('length', ('groups', 'sector', 'pair')), parts along dimension 1, may hold values from -1.1953125 to 1.1953125
- res_unary: bfloat16 [4, 8, 8, 8, 1024], P('length', ('groups', 'sector', 'pair')), parts along dimension 1, may hold values from -8 to 8
- res_labels: int32 [4, 8, 8, 1024], P('length', ('groups', 'sector', 'pair')), parts along dimension 1, may hold values from 0 to 7
- res_mask: int32 [4, 8, 8, 1024], P('length', ('groups', 'sector', 'pair')), parts along dimension 1, may hold values 0 or 1
Outputs:
- flag_grad: bfloat16 [4, 8, 32, 25, 1024], P('length', ('groups', 'sector', 'pair')), parts along dimension 1
- res_grad: bfloat16 [4, 8, 8, 25, 1024], P('length', ('groups', 'sector', 'pair')), parts along dimension 1
- helper_loss: float32 [4, 8, 16], P('length', ('groups', 'sector', 'pair')), parts along dimension 1
The draws below stay inside these ranges and needn't reach their ends.
There are 2 independent parts, one for each index of `groups`. The reference program is written for one: setup_inputs(seed, part) draws one part's arguments, and reference() takes and returns one part's arrays. A program takes and returns all parts, laid end to end along the dimension named above; each array names one. Nothing has to cross between parts.
Inputs may be any that keep to these rules, and one draw needn't show every extreme that they name: `dest_list`: entry j of a device's list is -1 exactly when its slot j holds no flagged tile, and the -1 entries come after all others; at most 8 entries of one device name the same destination. `slot_list`: for each index along sector and pair, each pair of a destination along length and a slot 0 to 15 is named by exactly one entry of the lists of the devices along length; an entry is -1 exactly where dest_list is -1.
All inputs are finite; a program needn't handle non-finite values. No bound on the sum of `flag_mask` or of `res_mask` on one device may be relied on, other than what follows from the above.
Results may differ from the reference program's by a relative error of at most 0.001.
Values may be sent and summed in bfloat16 or wider, within the bound.
A program may use at most 64 MiB of HBM per device.

```python
import jax
import jax.numpy as jnp
from jax import lax

CLASSES = 8
TAPS = 25
TILE = 32
ITERS = 3
FLAG_MAX = 32
RES = 8
PIX = 1024
NSP = 4
RECV = 16
N_LENGTH = 4
N_SECTOR = 2
N_PAIR = 2


def shuffle_slots(subkey):
    return jax.random.permutation(subkey, RECV)


def list_tables(key):
    device_count = N_LENGTH
    groups = N_SECTOR * N_PAIR

    def one_group(group_key):
        subkeys = jax.random.split(group_key, 6)
        spread = jax.random.randint(subkeys[0], (device_count // 2,), 0, RECV + 1)
        chosen = jax.random.randint(subkeys[1], (), 0, device_count // 2)
        spread = jnp.where(jnp.arange(device_count // 2) == chosen, RECV, spread)
        flip_sign = 2 * jax.random.randint(subkeys[2], (device_count // 2,), 0, 2) - 1
        paired = jnp.stack([RECV + flip_sign * spread, RECV - flip_sign * spread], axis=1).reshape(device_count)
        tile_loads = paired[jax.random.permutation(subkeys[3], device_count)]
        starts = jnp.cumsum(tile_loads) - tile_loads
        slot_order = jnp.arange(FLAG_MAX)
        global_index = starts[:, None] + slot_order[None, :]
        listed = slot_order[None, :] < tile_loads[:, None]
        rotation = jax.random.randint(subkeys[4], (), 0, device_count)
        target = (global_index + rotation) % device_count
        shuffles = jax.vmap(shuffle_slots)(jax.random.split(subkeys[5], device_count))
        slot_place = shuffles[target, jnp.minimum(global_index // device_count, RECV - 1)]
        return (jnp.where(listed, target, -1).astype(jnp.int32), jnp.where(listed, slot_place, -1).astype(jnp.int32))
    destinations, slot_names = jax.vmap(one_group)(jax.random.split(key, groups))
    return (jnp.transpose(destinations, (1, 0, 2)), jnp.transpose(slot_names, (1, 0, 2)))


def draw_dest_list(key, part):
    return list_tables(jax.random.fold_in(key, 11))[0]


def draw_slot_list(key, part):
    return list_tables(jax.random.fold_in(key, 11))[1]


def set_ends(array, own_key, low, high):
    shape = array.shape
    place = [jax.random.randint(jax.random.fold_in(own_key, axis), (), 0, shape[axis]) for axis in range(len(shape))]
    array = array.at[tuple(place)].set(low)
    longest = shape.index(max(shape))
    place[longest] = (place[longest] + 1) % shape[longest]
    return array.at[tuple(place)].set(high)


def block_levels(key, extent, cuts, least, top_value):
    gain, own = 1.0, jax.random.fold_in(key, 6)
    for dim, shards_of in cuts:
        draws = jnp.exp(jax.random.uniform(jax.random.fold_in(own, dim), (shards_of,), jnp.float32, least / len(cuts), top_value / len(cuts)))
        gain = gain * jnp.repeat(draws, extent[dim] // shards_of).reshape([-1 if axis == dim else 1 for axis in range(len(extent))])
    return gain


def gaussian(own_key, dims, width, bound, cuts=(), dtype=jnp.bfloat16):
    result = width * jax.random.normal(own_key, dims, jnp.float32)
    if cuts:
        result = result * block_levels(own_key, dims, cuts, -0.22, 0.18)
    return jnp.clip(result, -bound, bound).astype(dtype)


def setup_inputs(seed: int = 0, part: int = 0) -> dict:
    arg_keys = jax.random.split(jax.random.key(seed), 11)
    part_keys = jax.random.split(jax.random.fold_in(arg_keys[10], part), 11)
    flag_kernels = gaussian(part_keys[0], (N_LENGTH, NSP, FLAG_MAX, TAPS, PIX), 0.2, 1.1953125, ((0, 4), (1, 4)))
    flag_unary = gaussian(part_keys[1], (N_LENGTH, NSP, FLAG_MAX, CLASSES, PIX), 2.0, 8.0, ((0, 4), (1, 4)))
    flag_labels = set_ends(jax.random.randint(part_keys[2], (N_LENGTH, NSP, FLAG_MAX, PIX), 0, CLASSES), jax.random.fold_in(part_keys[2], 1), 0, CLASSES - 1).astype(jnp.int32)
    flag_mask = set_ends((jax.random.randint(part_keys[3], (N_LENGTH, NSP, FLAG_MAX, PIX), 0, 4) < 3).astype(jnp.int32), jax.random.fold_in(part_keys[3], 1), 0, 1)
    dest_list = draw_dest_list(jax.random.fold_in(jax.random.fold_in(arg_keys[10], part), 71), part)
    slot_list = draw_slot_list(jax.random.fold_in(jax.random.fold_in(arg_keys[10], part), 71), part)
    res_kernels = gaussian(part_keys[6], (N_LENGTH, NSP, RES, TAPS, PIX), 0.2, 1.1953125, ((0, 4), (1, 4)))
    res_unary = gaussian(part_keys[7], (N_LENGTH, NSP, RES, CLASSES, PIX), 2.0, 8.0, ((0, 4), (1, 4)))
    res_labels = set_ends(jax.random.randint(part_keys[8], (N_LENGTH, NSP, RES, PIX), 0, CLASSES), jax.random.fold_in(part_keys[8], 1), 0, CLASSES - 1).astype(jnp.int32)
    res_mask = set_ends((jax.random.randint(part_keys[9], (N_LENGTH, NSP, RES, PIX), 0, 4) < 3).astype(jnp.int32), jax.random.fold_in(part_keys[9], 1), 0, 1)
    return {"flag_kernels": flag_kernels, "flag_unary": flag_unary, "flag_labels": flag_labels, "flag_mask": flag_mask, "dest_list": dest_list, "slot_list": slot_list, "res_kernels": res_kernels, "res_unary": res_unary, "res_labels": res_labels, "res_mask": res_mask}


def normalize(logits):
    raised = jnp.exp(logits)
    return raised / lax.optimization_barrier(jnp.sum(raised, axis=0, keepdims=True))

def message(field_values, tap_weights):
    tile_side = TILE
    pixels = tile_side * tile_side
    margin = 2 * tile_side + 2
    padded = jnp.pad(field_values, ((0, 0), (margin, margin)))
    column = jnp.arange(pixels) % tile_side
    summed = jnp.zeros_like(field_values)
    tap_index = 0
    for row_step in range(-2, 3):
        for col_step in range(-2, 3):
            offset = row_step * tile_side + col_step
            shifted = lax.slice_in_dim(padded, margin + offset, margin + offset + pixels, axis=1)
            inside = ((column + col_step >= 0) & (column + col_step < tile_side)).astype(jnp.float32)
            summed = summed + (tap_weights[tap_index] * inside)[None, :] * shifted
            tap_index += 1
    return summed

def tile_objective(tap_weights, unary_terms, labels, weights):
    unary_terms = unary_terms.astype(jnp.float32)
    beliefs = normalize(unary_terms)
    logits = unary_terms
    for sweep_index in range(ITERS):
        logits = unary_terms + message(beliefs, tap_weights)
        if sweep_index + 1 < ITERS:
            beliefs = normalize(logits)
    summed = jnp.log(lax.optimization_barrier(jnp.sum(jnp.exp(logits), axis=0)))
    chosen = lax.optimization_barrier(jnp.sum(jnp.where(jnp.arange(CLASSES)[:, None] == labels[None, :], logits, 0.0), axis=0))
    return jnp.sum(weights * (summed - chosen))

def tile_work(tap_weights, unary_terms, labels, weights):
    total_value, gradient = jax.value_and_grad(tile_objective)(tap_weights.astype(jnp.float32), unary_terms, labels, weights)
    return (total_value / TILE, gradient.astype(jnp.bfloat16))

def batched(tap_weights, unary_terms, labels, weights, block_size):
    amount = tap_weights.shape[0]

    def compute_block(group_arrays):
        return jax.vmap(tile_work)(*group_arrays)
    shaped = tuple((member.reshape((amount // block_size, block_size) + member.shape[1:]) for member in (tap_weights, unary_terms, labels, weights)))
    losses, slopes = lax.map(compute_block, shaped)
    return (losses.reshape(amount), slopes.reshape((amount,) + slopes.shape[2:]))

def run_tiles(kernels, unary, labels, mask):
    leading = kernels.shape[:3]
    losses, slopes = batched(kernels.reshape((-1,) + kernels.shape[3:]), unary.reshape((-1,) + unary.shape[3:]), labels.reshape((-1, labels.shape[3])), mask.reshape((-1, mask.shape[3])).astype(jnp.float32), 16)
    return (losses.reshape(leading), slopes.reshape(kernels.shape))

def reference(flag_kernels, flag_unary, flag_labels, flag_mask, dest_list, slot_list, res_kernels, res_unary, res_labels, res_mask):
    flag_losses, flag_slopes = run_tiles(flag_kernels, flag_unary, flag_labels, flag_mask)
    resident_losses, resident_slopes = run_tiles(res_kernels, res_unary, res_labels, res_mask)
    is_listed = dest_list >= 0
    flag_grad = jnp.where(is_listed[..., None, None], flag_slopes, jnp.zeros_like(flag_slopes))
    leading = dest_list.shape
    row_index = jnp.where(is_listed, dest_list, N_LENGTH).astype(jnp.int32)
    columns = jnp.broadcast_to(jnp.arange(leading[1]).astype(jnp.int32)[None, :, None], leading)
    slot_index = jnp.where(is_listed, slot_list, 0).astype(jnp.int32)
    helper_loss = jnp.zeros((N_LENGTH, leading[1], RECV), jnp.float32).at[row_index, columns, slot_index].set(flag_losses, mode='drop')
    return (flag_grad, resident_slopes, helper_loss)
```

```python
import jax
import jax.numpy as jnp
from jax import lax
from jax.experimental import pallas as pl
from jax.experimental.pallas import tpu as pltpu
from jax.sharding import PartitionSpec as P

CLASSES = 8
FREE = CLASSES - 1
TAPS = 25
TILE = 32
ITERS = 3
RECV = 16
LANES = 128
COLS = 4
PAIR = 2


def total(values):
    while len(values) > 1:
        values = [sum(values[i : i + 2]) for i in range(0, len(values), 2)]
    return values[0]


def nt(x, y):
    return lax.dot_general(x, y, (((1,), (1,)), ((), ())), preferred_element_type=jnp.float32)


def turned(x, carry):
    return x if carry == 0 else pltpu.roll(x, 7 if carry > 0 else 1, 0)


def passed(x, carry, tiles):
    return x if carry == 0 else pltpu.roll(x, LANES - tiles if carry > 0 else tiles, 1)


def message(kern, field, q):
    acc = [[None] * COLS for _ in range(FREE)]
    for a in range(5):
        for p in range(COLS + 4):
            near = [field[c, q + a, p] for c in range(FREE)]
            for o in range(COLS):
                b = p - o
                if 0 <= b < 5:
                    k = kern[5 * a + b, q, o]
                    for c in range(FREE):
                        x = k * near[c]
                        acc[c][o] = x if acc[c][o] is None else acc[c][o] + x
    return acc


def put_row(field, c, row, values):
    for p in range(-2, COLS + 2):
        field[c, row, p + 2] = turned(values[p % COLS], p // COLS)


def put_edges(field, rows, tiles):
    for c in range(FREE):
        for e in range(2):
            for source, target, carry in ((e, rows + e, 1), (rows - 2 + e, e - 2, -1)):
                values = [passed(field[c, source + 2, p + 2], carry, tiles) for p in range(COLS)]
                put_row(field, c, target + 2, values)


def crf_kernel(dest_ref, k_ref, u_ref, lab_ref, mask_ref, grad_ref, loss_ref, *scratch):
    kf, kb, raw, un, tgt, prob, fld, gfld, out = scratch
    tiles = lab_ref.shape[0]
    groups = LANES // tiles
    rows = TILE // groups
    depth = rows * TILE
    lane = lax.broadcasted_iota(jnp.int32, (8, LANES), 1)
    sub = lax.broadcasted_iota(jnp.int32, (8, LANES), 0)
    one = jnp.ones((8, LANES), jnp.float32)
    width = max(depth, LANES)
    halves = width // depth
    chunks = groups // halves
    low = lane // tiles % 2 == 0

    def spot(x):
        return x // TILE * TILE + x % 8 * COLS + x // 8 % COLS

    row = lax.broadcasted_iota(jnp.int32, (width, width), 0)
    col = lax.broadcasted_iota(jnp.int32, (width, width), 1)
    gather = jnp.where(col == row // depth * depth + spot(row % depth), 1.0, 0.0)
    gather = gather.astype(jnp.bfloat16)
    row = lax.broadcasted_iota(jnp.int32, (chunks * tiles, LANES), 0)
    col = lax.broadcasted_iota(jnp.int32, (chunks * tiles, LANES), 1)
    scatter = (row % tiles == col % tiles) & (row // tiles == col // (tiles * halves))
    scatter = jnp.where(scatter, 1.0, 0.0).astype(jnp.bfloat16)

    def to_fields(part):
        pieces = [part(g) for g in range(chunks) for _ in range(halves)]
        turn = nt(gather, jnp.concatenate(pieces, axis=0).astype(jnp.bfloat16))
        both = lambda n: turn[8 * n : 8 * n + 8]
        regs = [
            both(n) if halves == 1 else jnp.where(low, both(n), both(n + rows * COLS))
            for n in range(rows * COLS)
        ]
        return [regs[q * COLS : (q + 1) * COLS] for q in range(rows)]

    def inside(a, b, q, o):
        ok = None
        if not 0 <= o + b < COLS:
            ok = sub > 0 if o + b < 0 else sub < 7
        if not 0 <= q + a < rows:
            near = lane >= tiles if q + a < 0 else lane < LANES - tiles
            ok = near if ok is None else ok & near
        return ok

    for a in range(-2, 3):
        for b in range(-2, 3):
            t = 5 * (a + 2) + b + 2
            regs = to_fields(
                lambda g: k_ref[0, 0, t, :, width * g : width * (g + 1)].astype(jnp.float32)
            )
            for q in range(rows):
                for o in range(COLS):
                    ok = inside(a, b, q, o)
                    if ok is not None:
                        regs[q][o] = jnp.where(ok, regs[q][o], 0.0)
                    kf[t, q, o] = regs[q][o]
            for q in range(rows):
                for o in range(COLS):
                    x = turned(regs[(q - a) % rows][(o - b) % COLS], (o - b) // COLS)
                    kb[TAPS - 1 - t, q, o] = passed(x, (q - a) // rows, tiles)

    @pl.loop(0, tiles)
    def _(j):
        for p in range(8):
            raw[p, pl.ds(pl.multiple_of(j * CLASSES, CLASSES), CLASSES), :] = u_ref[
                0, 0, j, :, LANES * p : LANES * (p + 1)
            ].astype(jnp.float32)

    def scores(c):
        def part(g):
            span = width // LANES
            rows_of = pl.ds(c, tiles, stride=CLASSES)
            return jnp.concatenate([raw[span * g + n, rows_of, :] for n in range(span)], axis=1)

        return to_fields(part)

    last = scores(FREE)
    for c in range(FREE):
        own = scores(c)
        for q in range(rows):
            for o in range(COLS):
                un[c, q, o] = own[q][o] - last[q][o]

    listed = []
    for n in range(tiles // 8):
        x = jnp.zeros((8, LANES), jnp.int32)
        for j in range(8):
            x = jnp.where(sub == j, dest_ref[8 * n + j], x)
        listed.append(x)
    listed = jnp.concatenate(listed, axis=0)
    listed = jnp.concatenate([listed] * (width // LANES), axis=1)

    def targets(g):
        part = slice(width * g, width * (g + 1))
        used = (mask_ref[:, part] == 1) & (listed >= 0)
        return jnp.where(used, lab_ref[:, part], CLASSES).astype(jnp.float32)

    for q, regs in enumerate(to_fields(targets)):
        for o in range(COLS):
            tgt[q, o] = regs[o]

    def soft(i, q, logits):
        values = [[None] * COLS for _ in range(FREE)]
        for o in range(COLS):
            raised = [jnp.exp(logits[c][o]) for c in range(FREE)]
            scale = 1.0 / total(raised + [one])
            for c in range(FREE):
                belief = raised[c] * scale
                prob[i, c, q, o] = belief
                values[c][o] = belief - scale
        for c in range(FREE):
            put_row(fld.at[i], c, q + 2, values[c])

    @pl.loop(0, rows)
    def _(q):
        soft(0, q, [[un[c, q, o] for o in range(COLS)] for c in range(FREE)])

    put_edges(fld.at[0], rows, tiles)

    def sweep(i, q):
        sent = message(kf, fld.at[i], q)
        return [[un[c, q, o] + sent[c][o] for o in range(COLS)] for c in range(FREE)]

    @pl.loop(0, ITERS - 1)
    def _(i):
        @pl.loop(0, rows // PAIR)
        def _(m):
            for n in range(PAIR):
                q = PAIR * m + n
                soft(i + 1, q, sweep(i, q))

        put_edges(fld.at[i + 1], rows, tiles)

    def final(m, partial):
        for n in range(PAIR):
            q = PAIR * m + n
            logits = sweep(ITERS - 1, q)
            values = [[None] * COLS for _ in range(FREE)]
            for o in range(COLS):
                raised = [jnp.exp(logits[c][o]) for c in range(FREE)]
                summed = total(raised + [one])
                labels = tgt[q, o]
                used = labels < CLASSES
                picked = [labels == c for c in range(FREE)]
                chosen = total([jnp.where(picked[c], logits[c][o], 0.0) for c in range(FREE)])
                partial = partial + jnp.where(used, jnp.log(summed) - chosen, 0.0)
                scale = jnp.where(used, 1.0 / summed, 0.0)
                for c in range(FREE):
                    values[c][o] = raised[c] * scale - jnp.where(picked[c], 1.0, 0.0)
            for c in range(FREE):
                put_row(gfld.at[ITERS - 1], c, q + 2, values[c])
        return partial

    loss_ref[...] = lax.fori_loop(
        0, rows // PAIR, final, jnp.zeros((8, LANES), jnp.float32)
    )
    put_edges(gfld.at[ITERS - 1], rows, tiles)

    @pl.loop(0, ITERS - 1)
    def _(n):
        i = ITERS - 1 - n

        @pl.loop(0, rows // PAIR)
        def _(m):
            for n in range(PAIR):
                q = PAIR * m + n
                back = message(kb, gfld.at[i], q)
                values = [[None] * COLS for _ in range(FREE)]
                for o in range(COLS):
                    mean = total(
                        [back[c][o] * fld[i, c, q + 2, o + 2] for c in range(FREE)]
                    )
                    for c in range(FREE):
                        values[c][o] = prob[i, c, q, o] * (back[c][o] - mean)
                for c in range(FREE):
                    put_row(gfld.at[i - 1], c, q + 2, values[c])

        @pl.when(i > 1)
        def _():
            put_edges(gfld.at[i - 1], rows, tiles)

    @pl.loop(0, rows * 5)
    def _(n):
        q, a = n // 5, n % 5
        acc = [[None] * COLS for _ in range(5)]
        for i in range(ITERS):
            for c in range(FREE):
                slope = [gfld[i, c, q + 2, o + 2] for o in range(COLS)]
                for p in range(COLS + 4):
                    x = fld[i, c, q + a, p]
                    for o in range(COLS):
                        b = p - o
                        if 0 <= b < 5:
                            y = slope[o] * x
                            acc[b][o] = y if acc[b][o] is None else acc[b][o] + y
        place = lane // tiles * rows + q + a - 2
        ok = (place >= 0) & (place < TILE)
        for b in range(5):
            for o in range(COLS):
                near = ok
                if not 0 <= o + b - 2 < COLS:
                    near = near & (sub > 0 if o + b < 2 else sub < 7)
                spots = pl.ds(q * TILE + o, 8, stride=COLS)
                out[5 * a + b, spots, :] = jnp.where(near, acc[b][o], 0.0)

    for t in range(TAPS):
        flat = out[t]
        if halves > 1:
            low = lax.broadcasted_iota(jnp.int32, flat.shape, 1) // tiles % 2 == 0
            flat = jnp.concatenate([jnp.where(low, flat, 0.0), jnp.where(low, 0.0, flat)], axis=0)
        back = nt(scatter, flat.astype(jnp.bfloat16)).astype(jnp.bfloat16)
        for g in range(chunks):
            grad_ref[0, 0, t, :, width * g : width * (g + 1)] = back[tiles * g : tiles * (g + 1)]


def crf(listed, kernels, unary, labels, mask):
    amount, taps, pixels = kernels.shape[2:]
    rows = TILE * amount // LANES
    kernels = jnp.swapaxes(kernels, 2, 3)
    vmem = pl.BlockSpec(memory_space=pltpu.VMEM)
    regs = lambda *lead: pltpu.VMEM((*lead, 8, LANES), jnp.float32)
    grad, loss = pl.pallas_call(
        crf_kernel,
        in_specs=[pl.BlockSpec(memory_space=pltpu.SMEM), vmem, vmem, vmem, vmem],
        out_specs=[vmem, vmem],
        scratch_shapes=[
            regs(taps, rows, COLS),
            regs(taps, rows, COLS),
            pltpu.VMEM((8, amount * CLASSES, LANES), jnp.float32),
            regs(FREE, rows, COLS),
            regs(rows, COLS),
            regs(ITERS, FREE, rows, COLS),
            regs(ITERS, FREE, rows + 4, COLS + 4),
            regs(ITERS, FREE, rows + 4, COLS + 4),
            pltpu.VMEM((taps, rows * TILE, LANES), jnp.float32),
        ],
        out_shape=[
            jax.ShapeDtypeStruct(kernels.shape, jnp.bfloat16),
            jax.ShapeDtypeStruct((8, LANES), jnp.float32),
        ],
        compiler_params=pltpu.CompilerParams(vmem_limit_bytes=44 * 1024 * 1024),
    )(listed, kernels, unary, labels[0, 0], mask[0, 0])
    return jnp.swapaxes(grad, 2, 3), loss.reshape(8, LANES // amount, amount)


def on_device(fk, fu, fl, fm, dest, slot, rk, ru, rl, rm):
    destinations, slots = dest[0, 0], slot[0, 0]
    flag_grad, partial = crf(destinations, fk, fu, fl, fm)
    count = lax.axis_size("length")
    losses = jnp.sum(partial, axis=(0, 1)) / TILE
    place = jnp.where(destinations >= 0, destinations * RECV + slots, -1)
    table = jnp.sum(
        jnp.where(place[None, :] == jnp.arange(count * RECV)[:, None], losses[None, :], 0.0), axis=1
    )
    got = lax.all_to_all(
        table.reshape(count, RECV), "length", split_axis=0, concat_axis=0, tiled=True
    )
    res_grad, _ = crf(jnp.zeros((rk.shape[2],), jnp.int32), rk, ru, rl, rm)
    return flag_grad, res_grad, jnp.sum(got, axis=0)[None, None]


def solution(mesh):
    tile_axes = ("groups", "sector", "pair")
    spec = lambda n: P("length", tile_axes, *([None] * n))
    return jax.shard_map(
        on_device,
        mesh=mesh,
        in_specs=(spec(3), spec(3), spec(2), spec(2), spec(1), spec(1), spec(3), spec(3), spec(2), spec(2)),
        out_specs=(spec(3), spec(3), spec(1)),
        check_vma=False,
    )
```

```python
import functools

import jax
import jax.numpy as jnp
from jax import lax
from jax.experimental import pallas as pl
from jax.experimental.pallas import tpu as pltpu
from jax.sharding import PartitionSpec as P

CLASSES = 8
FREE = CLASSES - 1
TAPS = 25
TILE = 32
ITERS = 3
RECV = 16
LANES = 128
COLS = 4
PAIR = 2


def total(values):
    while len(values) > 1:
        values = [sum(values[i : i + 2]) for i in range(0, len(values), 2)]
    return values[0]


def nt(x, y):
    return lax.dot_general(x, y, (((1,), (1,)), ((), ())), preferred_element_type=jnp.float32)


def turned(x, carry):
    return x if carry == 0 else pltpu.roll(x, 7 if carry > 0 else 1, 0)


def passed(x, carry, tiles):
    return x if carry == 0 else pltpu.roll(x, LANES - tiles if carry > 0 else tiles, 1)


def message(kern, field, q):
    acc = [[None] * COLS for _ in range(FREE)]
    for a in range(5):
        for p in range(COLS + 4):
            near = [field[c, q + a, p] for c in range(FREE)]
            for o in range(COLS):
                b = p - o
                if 0 <= b < 5:
                    k = kern[5 * a + b, q, o]
                    for c in range(FREE):
                        x = k * near[c]
                        acc[c][o] = x if acc[c][o] is None else acc[c][o] + x
    return acc


def put_row(field, c, row, values):
    for p in range(-2, COLS + 2):
        field[c, row, p + 2] = turned(values[p % COLS], p // COLS)


def put_edges(field, rows, tiles):
    for c in range(FREE):
        for e in range(2):
            for source, target, carry in ((e, rows + e, 1), (rows - 2 + e, e - 2, -1)):
                values = [passed(field[c, source + 2, p + 2], carry, tiles) for p in range(COLS)]
                put_row(field, c, target + 2, values)


def column(row):
    n = row.shape[1]
    own = lax.broadcasted_iota(jnp.int32, (n, n), 0) == lax.broadcasted_iota(jnp.int32, (n, n), 1)
    return jnp.sum(jnp.where(own, row, 0.0), axis=1, keepdims=True)


def tile_steps(after_loss, lists, k_ref, u_ref, lab_ref, mask_ref, grad_ref, loss_ref, dest_buf, scratch):
    kf, kb, raw, un, tgt, prob, fld, gfld, out, kbuf, ubuf, lab_buf, mask_buf, gbuf = scratch[:14]
    sems, out_sems = scratch[14:]
    lead = lists is not None
    tiles = lab_ref.shape[0]
    groups = LANES // tiles
    rows = TILE // groups
    depth = rows * TILE
    lane = lax.broadcasted_iota(jnp.int32, (8, LANES), 1)
    sub = lax.broadcasted_iota(jnp.int32, (8, LANES), 0)
    one = jnp.ones((8, LANES), jnp.float32)
    width = max(depth, LANES)
    halves = width // depth
    chunks = groups // halves
    low = lane // tiles % 2 == 0

    load_u = pltpu.make_async_copy(u_ref.at[0, 0], ubuf, sems.at[5])
    load_k = [
        pltpu.make_async_copy(
            k_ref.at[0, 0, pl.ds(5 * a, 5)], kbuf.at[pl.ds(5 * a, 5)], sems.at[a]
        )
        for a in range(5)
    ]
    load_lab = pltpu.make_async_copy(lab_ref, lab_buf, sems.at[6])
    load_mask = pltpu.make_async_copy(mask_ref, mask_buf, sems.at[7])
    for load in (load_u, *load_k, load_lab, load_mask):
        load.start()
    yield

    def spot(x):
        return x // TILE * TILE + x % 8 * COLS + x // 8 % COLS

    row = lax.broadcasted_iota(jnp.int32, (width, width), 0)
    col = lax.broadcasted_iota(jnp.int32, (width, width), 1)
    gather = jnp.where(col == row // depth * depth + spot(row % depth), 1.0, 0.0)
    gather = gather.astype(jnp.bfloat16)
    row = lax.broadcasted_iota(jnp.int32, (chunks * tiles, LANES), 0)
    col = lax.broadcasted_iota(jnp.int32, (chunks * tiles, LANES), 1)
    scatter = (row % tiles == col % tiles) & (row // tiles == col // (tiles * halves))
    scatter = jnp.where(scatter, 1.0, 0.0).astype(jnp.bfloat16)

    def to_fields(part):
        pieces = [part(g) for g in range(chunks) for _ in range(halves)]
        turn = nt(gather, jnp.concatenate(pieces, axis=0).astype(jnp.bfloat16))
        both = lambda n: turn[8 * n : 8 * n + 8]
        regs = [
            both(n) if halves == 1 else jnp.where(low, both(n), both(n + rows * COLS))
            for n in range(rows * COLS)
        ]
        return [regs[q * COLS : (q + 1) * COLS] for q in range(rows)]

    def inside(a, b, q, o):
        ok = None
        if not 0 <= o + b < COLS:
            ok = sub > 0 if o + b < 0 else sub < 7
        if not 0 <= q + a < rows:
            near = lane >= tiles if q + a < 0 else lane < LANES - tiles
            ok = near if ok is None else ok & near
        return ok

    load_u.wait()

    @pl.loop(0, tiles)
    def _(j):
        for p in range(8):
            raw[p, pl.ds(pl.multiple_of(j * CLASSES, CLASSES), CLASSES), :] = ubuf[
                j, :, LANES * p : LANES * (p + 1)
            ].astype(jnp.float32)

    def scores(c):
        def part(g):
            span = width // LANES
            rows_of = pl.ds(c, tiles, stride=CLASSES)
            return jnp.concatenate([raw[span * g + n, rows_of, :] for n in range(span)], axis=1)

        return to_fields(part)

    last = scores(FREE)
    for c in range(FREE):
        own = scores(c)
        for q in range(rows):
            for o in range(COLS):
                un[c, q, o] = own[q][o] - last[q][o]

    def soft(i, q, logits):
        values = [[None] * COLS for _ in range(FREE)]
        for o in range(COLS):
            raised = [jnp.exp(logits[c][o]) for c in range(FREE)]
            scale = 1.0 / total(raised + [one])
            for c in range(FREE):
                belief = raised[c] * scale
                prob[i, c, q, o] = belief
                values[c][o] = belief - scale
        for c in range(FREE):
            put_row(fld.at[i], c, q + 2, values[c])

    @pl.loop(0, rows)
    def _(q):
        soft(0, q, [[un[c, q, o] for o in range(COLS)] for c in range(FREE)])

    if lead:
        put_edges(fld.at[0], rows, tiles)
    yield

    for a in range(-2, 3):
        load_k[a + 2].wait()
        for b in range(-2, 3):
            t = 5 * (a + 2) + b + 2
            regs = to_fields(
                lambda g: kbuf[t, :, width * g : width * (g + 1)].astype(jnp.float32)
            )
            for q in range(rows):
                for o in range(COLS):
                    ok = inside(a, b, q, o)
                    if ok is not None:
                        regs[q][o] = jnp.where(ok, regs[q][o], 0.0)
                    kf[t, q, o] = regs[q][o]
            for q in range(rows):
                for o in range(COLS):
                    x = turned(regs[(q - a) % rows][(o - b) % COLS], (o - b) // COLS)
                    kb[TAPS - 1 - t, q, o] = passed(x, (q - a) // rows, tiles)

    load_lab.wait()
    load_mask.wait()
    if lead:
        for load in lists:
            load.wait()
        listed = column(dest_buf[...].astype(jnp.float32)) >= 0.0
        listed = jnp.broadcast_to(jnp.where(listed, 1, 0), (tiles, width))

    def targets(g):
        part = slice(width * g, width * (g + 1))
        used = mask_buf[:, part] == 1
        if lead:
            used = used & (listed == 1)
        return jnp.where(used, lab_buf[:, part], CLASSES).astype(jnp.float32)

    for q, regs in enumerate(to_fields(targets)):
        for o in range(COLS):
            tgt[q, o] = regs[o]

    yield

    def pairs(work):
        if rows > PAIR:
            pl.loop(0, rows // PAIR)(work)
        else:
            work(0)

    def sweep(i, q):
        sent = message(kf, fld.at[i], q)
        return [[un[c, q, o] + sent[c][o] for o in range(COLS)] for c in range(FREE)]

    def forward(i, m):
        for n in range(PAIR):
            q = PAIR * m + n
            soft(i + 1, q, sweep(i, q))

    def final(m):
        for n in range(PAIR):
            q = PAIR * m + n
            logits = sweep(ITERS - 1, q)
            values = [[None] * COLS for _ in range(FREE)]
            for o in range(COLS):
                raised = [jnp.exp(logits[c][o]) for c in range(FREE)]
                summed = total(raised + [one])
                labels = tgt[q, o]
                used = labels < CLASSES
                picked = [labels == c for c in range(FREE)]
                if loss_ref is not None:
                    chosen = total([jnp.where(picked[c], logits[c][o], 0.0) for c in range(FREE)])
                    loss_ref[...] += jnp.where(used, jnp.log(summed) - chosen, 0.0)
                scale = jnp.where(used, 1.0 / summed, 0.0)
                for c in range(FREE):
                    values[c][o] = raised[c] * scale - jnp.where(picked[c], 1.0, 0.0)
            for c in range(FREE):
                put_row(gfld.at[ITERS - 1], c, q + 2, values[c])

    def backward(i, m):
        for n in range(PAIR):
            q = PAIR * m + n
            back = message(kb, gfld.at[i], q)
            values = [[None] * COLS for _ in range(FREE)]
            for o in range(COLS):
                mean = total([back[c][o] * fld[i, c, q + 2, o + 2] for c in range(FREE)])
                for c in range(FREE):
                    values[c][o] = prob[i, c, q, o] * (back[c][o] - mean)
            for c in range(FREE):
                put_row(gfld.at[i - 1], c, q + 2, values[c])

    if loss_ref is not None:
        loss_ref[...] = jnp.zeros((8, LANES), jnp.float32)
    works = [
        (functools.partial(forward, 0), fld.at[0]),
        (functools.partial(forward, 1), fld.at[1]),
        (final, fld.at[2]),
        (functools.partial(backward, 2), gfld.at[2]),
        (functools.partial(backward, 1), gfld.at[1]),
    ]
    for n, (work, field) in enumerate(works):
        if not lead:
            put_edges(field, rows, tiles)
        pairs(work)
        if lead and n + 1 < len(works):
            put_edges(works[n + 1][1], rows, tiles)
        if lead and work is final:
            after_loss()
        yield

    def store(a):
        part = pl.ds(5 * a, 5)
        return pltpu.make_async_copy(gbuf.at[part], grad_ref.at[0, 0, part], out_sems.at[a])

    @pl.loop(0, 5)
    def _(a):
        @pl.loop(0, rows // PAIR)
        def _(m):
            def step(i, flat):
                flat = list(flat)
                for c in range(FREE):
                    for r in range(PAIR):
                        q = PAIR * m + r
                        slope = [gfld[i, c, q + 2, o + 2] for o in range(COLS)]
                        for p in range(COLS + 4):
                            x = fld[i, c, q + a, p]
                            for o in range(COLS):
                                b = p - o
                                if 0 <= b < 5:
                                    n = (r * 5 + b) * COLS + o
                                    flat[n] = flat[n] + slope[o] * x
                return flat

            zeros = [jnp.zeros((8, LANES), jnp.float32)] * (PAIR * 5 * COLS)
            flat = lax.fori_loop(0, ITERS, step, zeros)
            for r in range(PAIR):
                q = PAIR * m + r
                place = lane // tiles * rows + q + a - 2
                ok = (place >= 0) & (place < TILE)
                for b in range(5):
                    for o in range(COLS):
                        near = ok
                        if not 0 <= o + b - 2 < COLS:
                            near = near & (sub > 0 if o + b < 2 else sub < 7)
                        spots = pl.ds(q * TILE + o, 8, stride=COLS)
                        x = flat[(r * 5 + b) * COLS + o]
                        out[5 * a + b, spots, :] = jnp.where(near, x, 0.0)

    yield
    for t in range(TAPS):
        flat = out[t]
        if halves > 1:
            even = lax.broadcasted_iota(jnp.int32, flat.shape, 1) // tiles % 2 == 0
            flat = jnp.concatenate([jnp.where(even, flat, 0.0), jnp.where(even, 0.0, flat)], axis=0)
        back = nt(scatter, flat.astype(jnp.bfloat16)).astype(jnp.bfloat16)
        for g in range(chunks):
            gbuf[t, :, width * g : width * (g + 1)] = back[tiles * g : tiles * (g + 1)]
        if t % 5 == 4:
            store(t // 5).start()
    yield
    for a in range(5):
        store(a).wait()


def crf_kernel(*refs):
    dest_ref, slot_ref, flagged, resident = refs[0], refs[1], refs[2:6], refs[6:10]
    flag_grad, res_grad, table_ref = refs[10:13]
    loss_buf, dest_buf, slot_buf, table_buf, list_sems = refs[13:18]
    scratch = refs[18:]
    half = len(scratch) // 2
    lists = [
        pltpu.make_async_copy(dest_ref, dest_buf, list_sems.at[0]),
        pltpu.make_async_copy(slot_ref, slot_buf, list_sems.at[1]),
    ]
    for load in lists:
        load.start()
    leave = pltpu.make_async_copy(table_buf, table_ref, list_sems.at[2])

    def tabulate():
        amount = dest_buf.shape[1]
        row = jnp.sum(loss_buf[...], axis=0, keepdims=True)
        shift = amount
        while shift < LANES:
            row = row + pltpu.roll(row, shift, 1)
            shift *= 2
        losses = column(row[:, :amount]) / TILE
        dests = column(dest_buf[...].astype(jnp.float32))
        slots = column(slot_buf[...].astype(jnp.float32))
        place = lax.broadcasted_iota(jnp.int32, (amount, LANES), 1).astype(jnp.float32)
        for d in range(table_buf.shape[0]):
            picked = jnp.where((dests == d) & (slots == place), losses, 0.0)
            table_buf[d] = jnp.broadcast_to(jnp.sum(picked, axis=0, keepdims=True), (8, LANES))
        leave.start()

    runs = [
        tile_steps(tabulate, lists, *flagged, flag_grad, loss_buf, dest_buf, scratch[:half]),
        tile_steps(None, None, *resident, res_grad, None, None, scratch[half:]),
    ]
    while runs:
        runs = [run for run in runs if next(run, True) is None]
    leave.wait()


def exchange_kernel(count, table_ref, help_ref, heard, send_sems, recv_sems, own_sem):
    me = lax.axis_index("length")
    peers = [(me + k) % count for k in range(1, count)]
    barrier = pltpu.get_barrier_semaphore()
    for peer in peers:
        pl.semaphore_signal(
            barrier, inc=1, device_id={"length": peer}, device_id_type=pl.DeviceIdType.MESH
        )
    own = pltpu.make_async_copy(table_ref.at[me], heard.at[count - 1], own_sem)
    own.start()
    pl.semaphore_wait(barrier, count - 1)
    sends = [
        pltpu.make_async_remote_copy(
            src_ref=table_ref.at[peer],
            dst_ref=heard.at[k],
            send_sem=send_sems.at[k],
            recv_sem=recv_sems.at[k],
            device_id={"length": peer},
            device_id_type=pl.DeviceIdType.MESH,
        )
        for k, peer in enumerate(peers)
    ]
    for send in sends:
        send.start()
    own.wait()
    summed = heard[count - 1]
    for k, send in enumerate(sends):
        send.wait()
        summed = summed + heard[k]
    help_ref[...] = summed


def scratch_for(kernels):
    taps, amount, pixels = kernels.shape[2:]
    rows = TILE * amount // LANES
    regs = lambda *lead: pltpu.VMEM((*lead, 8, LANES), jnp.float32)
    return [
        regs(taps, rows, COLS),
        regs(taps, rows, COLS),
        pltpu.VMEM((8, amount * CLASSES, LANES), jnp.float32),
        regs(FREE, rows, COLS),
        regs(rows, COLS),
        regs(ITERS, FREE, rows, COLS),
        regs(ITERS, FREE, rows + 4, COLS + 4),
        regs(ITERS, FREE, rows + 4, COLS + 4),
        pltpu.VMEM((taps, rows * TILE, LANES), jnp.float32),
        pltpu.VMEM((taps, amount, pixels), jnp.bfloat16),
        pltpu.VMEM((amount, CLASSES, pixels), jnp.bfloat16),
        pltpu.VMEM((amount, pixels), jnp.int32),
        pltpu.VMEM((amount, pixels), jnp.int32),
        pltpu.VMEM((taps, amount, pixels), jnp.bfloat16),
        pltpu.SemaphoreType.DMA((8,)),
        pltpu.SemaphoreType.DMA((5,)),
    ]


def on_device(fk, fu, fl, fm, dest, slot, rk, ru, rl, rm):
    count = lax.axis_size("length")
    fk, rk = jnp.swapaxes(fk, 2, 3), jnp.swapaxes(rk, 2, 3)
    hbm = pl.BlockSpec(memory_space=pltpu.HBM)
    vmem = pl.BlockSpec(memory_space=pltpu.VMEM)
    tile_field = jax.ShapeDtypeStruct((8, LANES), jnp.float32)
    listed = dest.shape[2]
    field = (8, LANES)
    flag_grad, res_grad, table = pl.pallas_call(
        crf_kernel,
        in_specs=[hbm] * 10,
        out_specs=[hbm] * 3,
        scratch_shapes=[
            pltpu.VMEM(field, jnp.float32),
            pltpu.VMEM((1, listed), jnp.int32),
            pltpu.VMEM((1, listed), jnp.int32),
            pltpu.VMEM((count, *field), jnp.float32),
            pltpu.SemaphoreType.DMA((3,)),
            *scratch_for(fk),
            *scratch_for(rk),
        ],
        out_shape=[
            jax.ShapeDtypeStruct(fk.shape, jnp.bfloat16),
            jax.ShapeDtypeStruct(rk.shape, jnp.bfloat16),
            jax.ShapeDtypeStruct((count, *field), jnp.float32),
        ],
        compiler_params=pltpu.CompilerParams(vmem_limit_bytes=63_400_000),
    )(dest[0], slot[0], fk, fu, fl[0, 0], fm[0, 0], rk, ru, rl[0, 0], rm[0, 0])
    helped = pl.pallas_call(
        functools.partial(exchange_kernel, count),
        in_specs=[hbm],
        out_specs=vmem,
        scratch_shapes=[
            pltpu.VMEM((count, *field), jnp.float32),
            pltpu.SemaphoreType.DMA((count - 1,)),
            pltpu.SemaphoreType.DMA((count - 1,)),
            pltpu.SemaphoreType.DMA,
        ],
        out_shape=jax.ShapeDtypeStruct(field, jnp.float32),
        compiler_params=pltpu.CompilerParams(
            collective_id=0, has_side_effects=True, vmem_limit_bytes=4 * 1024 * 1024
        ),
    )(table)
    return jnp.swapaxes(flag_grad, 2, 3), jnp.swapaxes(res_grad, 2, 3), helped[None, :1, :RECV]


def solution(mesh):
    tile_axes = ("groups", "sector", "pair")
    spec = lambda n: P("length", tile_axes, *([None] * n))
    return jax.shard_map(
        on_device,
        mesh=mesh,
        in_specs=(spec(3), spec(3), spec(2), spec(2), spec(1), spec(1), spec(3), spec(3), spec(2), spec(2)),
        out_specs=(spec(3), spec(3), spec(1)),
        check_vma=False,
    )
```

```python
import functools

import jax
import jax.numpy as jnp
from jax import lax
from jax.experimental import pallas as pl
from jax.experimental.pallas import tpu as pltpu
from jax.sharding import PartitionSpec as P

CLASSES = 8
FREE = CLASSES - 1
TAPS = 25
TILE = 32
ITERS = 3
RECV = 16
LANES = 128
COLS = 4
PAIR = 2


def total(values):
    while len(values) > 1:
        values = [sum(values[i : i + 2]) for i in range(0, len(values), 2)]
    return values[0]


def nt(x, y):
    return lax.dot_general(x, y, (((1,), (1,)), ((), ())), preferred_element_type=jnp.float32)


def turned(x, carry):
    return x if carry == 0 else pltpu.roll(x, 7 if carry > 0 else 1, 0)


def passed(x, carry, tiles):
    return x if carry == 0 else pltpu.roll(x, LANES - tiles if carry > 0 else tiles, 1)


def message(kern, field, q):
    acc = [[None] * COLS for _ in range(FREE)]
    for a in range(5):
        for p in range(COLS + 4):
            near = [field[c, q + a, p] for c in range(FREE)]
            for o in range(COLS):
                b = p - o
                if 0 <= b < 5:
                    k = kern[5 * a + b, q, o]
                    for c in range(FREE):
                        x = k * near[c]
                        acc[c][o] = x if acc[c][o] is None else acc[c][o] + x
    return acc


def put_row(field, c, row, values):
    for p in range(-2, COLS + 2):
        field[c, row, p + 2] = turned(values[p % COLS], p // COLS)


def put_edges(field, rows, tiles):
    for c in range(FREE):
        for e in range(2):
            for source, target, carry in ((e, rows + e, 1), (rows - 2 + e, e - 2, -1)):
                values = [passed(field[c, source + 2, p + 2], carry, tiles) for p in range(COLS)]
                put_row(field, c, target + 2, values)


def column(row):
    n = row.shape[1]
    own = lax.broadcasted_iota(jnp.int32, (n, n), 0) == lax.broadcasted_iota(jnp.int32, (n, n), 1)
    return jnp.sum(jnp.where(own, row, 0.0), axis=1, keepdims=True)


def tile_steps(after_loss, lists, k_ref, u_ref, lab_ref, mask_ref, grad_ref, loss_ref, dest_buf, scratch):
    kf, kb, raw, un, tgt, prob, fld, gfld, out, kbuf, ubuf, lab_buf, mask_buf, gbuf = scratch[:14]
    sems, out_sems = scratch[14:]
    lead = lists is not None
    tiles = lab_ref.shape[0]
    groups = LANES // tiles
    rows = TILE // groups
    depth = rows * TILE
    lane = lax.broadcasted_iota(jnp.int32, (8, LANES), 1)
    sub = lax.broadcasted_iota(jnp.int32, (8, LANES), 0)
    one = jnp.ones((8, LANES), jnp.float32)
    width = max(depth, LANES)
    halves = width // depth
    chunks = groups // halves
    low = lane // tiles % 2 == 0

    load_u = pltpu.make_async_copy(u_ref.at[0, 0], ubuf, sems.at[5])
    load_k = [
        pltpu.make_async_copy(
            k_ref.at[0, 0, pl.ds(5 * a, 5)], kbuf.at[pl.ds(5 * a, 5)], sems.at[a]
        )
        for a in range(5)
    ]
    load_lab = pltpu.make_async_copy(lab_ref, lab_buf, sems.at[6])
    load_mask = pltpu.make_async_copy(mask_ref, mask_buf, sems.at[7])
    for load in (load_u, *load_k, load_lab, load_mask):
        load.start()
    yield

    def spot(x):
        return x // TILE * TILE + x % 8 * COLS + x // 8 % COLS

    row = lax.broadcasted_iota(jnp.int32, (width, width), 0)
    col = lax.broadcasted_iota(jnp.int32, (width, width), 1)
    gather = jnp.where(col == row // depth * depth + spot(row % depth), 1.0, 0.0)
    gather = gather.astype(jnp.bfloat16)
    row = lax.broadcasted_iota(jnp.int32, (chunks * tiles, LANES), 0)
    col = lax.broadcasted_iota(jnp.int32, (chunks * tiles, LANES), 1)
    scatter = (row % tiles == col % tiles) & (row // tiles == col // (tiles * halves))
    scatter = jnp.where(scatter, 1.0, 0.0).astype(jnp.bfloat16)

    def to_fields(part):
        pieces = [part(g) for g in range(chunks) for _ in range(halves)]
        turn = nt(gather, jnp.concatenate(pieces, axis=0).astype(jnp.bfloat16))
        both = lambda n: turn[8 * n : 8 * n + 8]
        regs = [
            both(n) if halves == 1 else jnp.where(low, both(n), both(n + rows * COLS))
            for n in range(rows * COLS)
        ]
        return [regs[q * COLS : (q + 1) * COLS] for q in range(rows)]

    def inside(a, b, q, o):
        ok = None
        if not 0 <= o + b < COLS:
            ok = sub > 0 if o + b < 0 else sub < 7
        if not 0 <= q + a < rows:
            near = lane >= tiles if q + a < 0 else lane < LANES - tiles
            ok = near if ok is None else ok & near
        return ok

    load_u.wait()

    @pl.loop(0, tiles)
    def _(j):
        for p in range(8):
            raw[p, pl.ds(pl.multiple_of(j * CLASSES, CLASSES), CLASSES), :] = ubuf[
                j, :, LANES * p : LANES * (p + 1)
            ].astype(jnp.float32)

    def scores(c):
        def part(g):
            span = width // LANES
            rows_of = pl.ds(c, tiles, stride=CLASSES)
            return jnp.concatenate([raw[span * g + n, rows_of, :] for n in range(span)], axis=1)

        return to_fields(part)

    last = scores(FREE)
    for c in range(FREE):
        own = scores(c)
        for q in range(rows):
            for o in range(COLS):
                un[c, q, o] = own[q][o] - last[q][o]

    def soft(i, q, logits):
        values = [[None] * COLS for _ in range(FREE)]
        for o in range(COLS):
            raised = [jnp.exp(logits[c][o]) for c in range(FREE)]
            scale = 1.0 / total(raised + [one])
            for c in range(FREE):
                belief = raised[c] * scale
                prob[i, c, q, o] = belief
                values[c][o] = belief - scale
        for c in range(FREE):
            put_row(fld.at[i], c, q + 2, values[c])

    @pl.loop(0, rows)
    def _(q):
        soft(0, q, [[un[c, q, o] for o in range(COLS)] for c in range(FREE)])

    if lead:
        put_edges(fld.at[0], rows, tiles)
    yield

    for a in range(-2, 3):
        load_k[a + 2].wait()
        for b in range(-2, 3):
            t = 5 * (a + 2) + b + 2
            regs = to_fields(
                lambda g: kbuf[t, :, width * g : width * (g + 1)].astype(jnp.float32)
            )
            for q in range(rows):
                for o in range(COLS):
                    ok = inside(a, b, q, o)
                    if ok is not None:
                        regs[q][o] = jnp.where(ok, regs[q][o], 0.0)
                    kf[t, q, o] = regs[q][o]
            for q in range(rows):
                for o in range(COLS):
                    x = turned(regs[(q - a) % rows][(o - b) % COLS], (o - b) // COLS)
                    kb[TAPS - 1 - t, q, o] = passed(x, (q - a) // rows, tiles)

    load_lab.wait()
    load_mask.wait()
    if lead:
        for load in lists:
            load.wait()
        listed = column(dest_buf[...].astype(jnp.float32)) >= 0.0
        listed = jnp.broadcast_to(jnp.where(listed, 1, 0), (tiles, width))

    def targets(g):
        part = slice(width * g, width * (g + 1))
        used = mask_buf[:, part] == 1
        if lead:
            used = used & (listed == 1)
        return jnp.where(used, lab_buf[:, part], CLASSES).astype(jnp.float32)

    for q, regs in enumerate(to_fields(targets)):
        for o in range(COLS):
            tgt[q, o] = regs[o]

    yield

    def pairs(work):
        if rows > PAIR:
            pl.loop(0, rows // PAIR)(work)
        else:
            work(0)

    def sweep(i, q):
        sent = message(kf, fld.at[i], q)
        return [[un[c, q, o] + sent[c][o] for o in range(COLS)] for c in range(FREE)]

    def forward(i, m):
        for n in range(PAIR):
            q = PAIR * m + n
            soft(i + 1, q, sweep(i, q))

    def final(m):
        for n in range(PAIR):
            q = PAIR * m + n
            logits = sweep(ITERS - 1, q)
            values = [[None] * COLS for _ in range(FREE)]
            for o in range(COLS):
                raised = [jnp.exp(logits[c][o]) for c in range(FREE)]
                summed = total(raised + [one])
                labels = tgt[q, o]
                used = labels < CLASSES
                picked = [labels == c for c in range(FREE)]
                if loss_ref is not None:
                    chosen = total([jnp.where(picked[c], logits[c][o], 0.0) for c in range(FREE)])
                    loss_ref[...] += jnp.where(used, jnp.log(summed) - chosen, 0.0)
                scale = jnp.where(used, 1.0 / summed, 0.0)
                for c in range(FREE):
                    values[c][o] = raised[c] * scale - jnp.where(picked[c], 1.0, 0.0)
            for c in range(FREE):
                put_row(gfld.at[ITERS - 1], c, q + 2, values[c])

    def backward(i, m):
        for n in range(PAIR):
            q = PAIR * m + n
            back = message(kb, gfld.at[i], q)
            values = [[None] * COLS for _ in range(FREE)]
            for o in range(COLS):
                mean = total([back[c][o] * fld[i, c, q + 2, o + 2] for c in range(FREE)])
                for c in range(FREE):
                    values[c][o] = prob[i, c, q, o] * (back[c][o] - mean)
            for c in range(FREE):
                put_row(gfld.at[i - 1], c, q + 2, values[c])

    if loss_ref is not None:
        loss_ref[...] = jnp.zeros((8, LANES), jnp.float32)
    works = [
        (functools.partial(forward, 0), fld.at[0]),
        (functools.partial(forward, 1), fld.at[1]),
        (final, fld.at[2]),
        (functools.partial(backward, 2), gfld.at[2]),
        (functools.partial(backward, 1), gfld.at[1]),
    ]
    for n, (work, field) in enumerate(works):
        if not lead:
            put_edges(field, rows, tiles)
        pairs(work)
        if lead and n + 1 < len(works):
            put_edges(works[n + 1][1], rows, tiles)
        if lead and work is final:
            after_loss()
        yield

    def store(a):
        part = pl.ds(5 * a, 5)
        return pltpu.make_async_copy(gbuf.at[part], grad_ref.at[0, 0, part], out_sems.at[a])

    @pl.loop(0, 5)
    def _(a):
        @pl.loop(0, rows // PAIR)
        def _(m):
            def step(i, flat):
                flat = list(flat)
                for c in range(FREE):
                    for r in range(PAIR):
                        q = PAIR * m + r
                        slope = [gfld[i, c, q + 2, o + 2] for o in range(COLS)]
                        for p in range(COLS + 4):
                            x = fld[i, c, q + a, p]
                            for o in range(COLS):
                                b = p - o
                                if 0 <= b < 5:
                                    n = (r * 5 + b) * COLS + o
                                    flat[n] = flat[n] + slope[o] * x
                return flat

            zeros = [jnp.zeros((8, LANES), jnp.float32)] * (PAIR * 5 * COLS)
            flat = lax.fori_loop(0, ITERS, step, zeros)
            for r in range(PAIR):
                q = PAIR * m + r
                place = lane // tiles * rows + q + a - 2
                ok = (place >= 0) & (place < TILE)
                for b in range(5):
                    for o in range(COLS):
                        near = ok
                        if not 0 <= o + b - 2 < COLS:
                            near = near & (sub > 0 if o + b < 2 else sub < 7)
                        spots = pl.ds(q * TILE + o, 8, stride=COLS)
                        x = flat[(r * 5 + b) * COLS + o]
                        out[5 * a + b, spots, :] = jnp.where(near, x, 0.0)

    yield
    for t in range(TAPS):
        flat = out[t]
        if halves > 1:
            even = lax.broadcasted_iota(jnp.int32, flat.shape, 1) // tiles % 2 == 0
            flat = jnp.concatenate([jnp.where(even, flat, 0.0), jnp.where(even, 0.0, flat)], axis=0)
        back = nt(scatter, flat.astype(jnp.bfloat16)).astype(jnp.bfloat16)
        for g in range(chunks):
            gbuf[t, :, width * g : width * (g + 1)] = back[tiles * g : tiles * (g + 1)]
        if t % 5 == 4:
            store(t // 5).start()
    yield
    for a in range(5):
        store(a).wait()


def flagged_kernel(*refs):
    dest_ref, slot_ref, flagged = refs[0], refs[1], refs[2:6]
    flag_grad, table_ref = refs[6:8]
    loss_buf, dest_buf, slot_buf, table_buf, list_sems = refs[8:13]
    scratch = refs[13:]
    lists = [
        pltpu.make_async_copy(dest_ref, dest_buf, list_sems.at[0]),
        pltpu.make_async_copy(slot_ref, slot_buf, list_sems.at[1]),
    ]
    for load in lists:
        load.start()
    leave = pltpu.make_async_copy(table_buf, table_ref, list_sems.at[2])

    def tabulate():
        amount = dest_buf.shape[1]
        row = jnp.sum(loss_buf[...], axis=0, keepdims=True)
        shift = amount
        while shift < LANES:
            row = row + pltpu.roll(row, shift, 1)
            shift *= 2
        losses = column(row[:, :amount]) / TILE
        dests = column(dest_buf[...].astype(jnp.float32))
        slots = column(slot_buf[...].astype(jnp.float32))
        place = lax.broadcasted_iota(jnp.int32, (amount, LANES), 1).astype(jnp.float32)
        for d in range(table_buf.shape[0]):
            picked = jnp.where((dests == d) & (slots == place), losses, 0.0)
            table_buf[d] = jnp.broadcast_to(jnp.sum(picked, axis=0, keepdims=True), (8, LANES))
        leave.start()

    steps = tile_steps(tabulate, lists, *flagged, flag_grad, loss_buf, dest_buf, scratch)
    for _ in steps:
        pass
    leave.wait()


def resident_kernel(count, table_ref, *refs):
    resident, res_grad, help_ref = refs[:4], refs[4], refs[5]
    heard, send_sems, recv_sems, own_sem = refs[6:10]
    me = lax.axis_index("length")
    peers = [(me + k) % count for k in range(1, count)]
    barrier = pltpu.get_barrier_semaphore()
    for peer in peers:
        pl.semaphore_signal(
            barrier, inc=1, device_id={"length": peer}, device_id_type=pl.DeviceIdType.MESH
        )
    own = pltpu.make_async_copy(table_ref.at[me], heard.at[count - 1], own_sem)
    sends = [
        pltpu.make_async_remote_copy(
            src_ref=table_ref.at[peer],
            dst_ref=heard.at[k],
            send_sem=send_sems.at[k],
            recv_sem=recv_sems.at[k],
            device_id={"length": peer},
            device_id_type=pl.DeviceIdType.MESH,
        )
        for k, peer in enumerate(peers)
    ]
    steps = tile_steps(None, None, *resident, res_grad, None, None, refs[10:])
    for n, _ in enumerate(steps):
        if n == 3:
            own.start()
            pl.semaphore_wait(barrier, count - 1)
            for send in sends:
                send.start()
    own.wait()
    summed = heard[count - 1]
    for k, send in enumerate(sends):
        send.wait()
        summed = summed + heard[k]
    help_ref[...] = summed[0:1, :RECV]


def scratch_for(kernels):
    taps, amount, pixels = kernels.shape[2:]
    rows = TILE * amount // LANES
    regs = lambda *lead: pltpu.VMEM((*lead, 8, LANES), jnp.float32)
    return [
        regs(taps, rows, COLS),
        regs(taps, rows, COLS),
        pltpu.VMEM((8, amount * CLASSES, LANES), jnp.float32),
        regs(FREE, rows, COLS),
        regs(rows, COLS),
        regs(ITERS, FREE, rows, COLS),
        regs(ITERS, FREE, rows + 4, COLS + 4),
        regs(ITERS, FREE, rows + 4, COLS + 4),
        pltpu.VMEM((taps, rows * TILE, LANES), jnp.float32),
        pltpu.VMEM((taps, amount, pixels), jnp.bfloat16),
        pltpu.VMEM((amount, CLASSES, pixels), jnp.bfloat16),
        pltpu.VMEM((amount, pixels), jnp.int32),
        pltpu.VMEM((amount, pixels), jnp.int32),
        pltpu.VMEM((taps, amount, pixels), jnp.bfloat16),
        pltpu.SemaphoreType.DMA((8,)),
        pltpu.SemaphoreType.DMA((5,)),
    ]


def on_device(fk, fu, fl, fm, dest, slot, rk, ru, rl, rm):
    count = lax.axis_size("length")
    fk, rk = jnp.swapaxes(fk, 2, 3), jnp.swapaxes(rk, 2, 3)
    hbm = pl.BlockSpec(memory_space=pltpu.HBM)
    vmem = pl.BlockSpec(memory_space=pltpu.VMEM)
    tile_field = jax.ShapeDtypeStruct((8, LANES), jnp.float32)
    listed = dest.shape[2]
    field = (8, LANES)
    flag_grad, table = pl.pallas_call(
        flagged_kernel,
        in_specs=[hbm] * 6,
        out_specs=[hbm] * 2,
        scratch_shapes=[
            pltpu.VMEM(field, jnp.float32),
            pltpu.VMEM((1, listed), jnp.int32),
            pltpu.VMEM((1, listed), jnp.int32),
            pltpu.VMEM((count, *field), jnp.float32),
            pltpu.SemaphoreType.DMA((3,)),
            *scratch_for(fk),
        ],
        out_shape=[
            jax.ShapeDtypeStruct(fk.shape, jnp.bfloat16),
            jax.ShapeDtypeStruct((count, *field), jnp.float32),
        ],
        compiler_params=pltpu.CompilerParams(vmem_limit_bytes=63_400_000),
    )(dest[0], slot[0], fk, fu, fl[0, 0], fm[0, 0])
    res_grad, helped = pl.pallas_call(
        functools.partial(resident_kernel, count),
        in_specs=[hbm] * 5,
        out_specs=[hbm, vmem],
        scratch_shapes=[
            pltpu.VMEM((count, *field), jnp.float32),
            pltpu.SemaphoreType.DMA((count - 1,)),
            pltpu.SemaphoreType.DMA((count - 1,)),
            pltpu.SemaphoreType.DMA,
            *scratch_for(rk),
        ],
        out_shape=[
            jax.ShapeDtypeStruct(rk.shape, jnp.bfloat16),
            jax.ShapeDtypeStruct((1, RECV), jnp.float32),
        ],
        compiler_params=pltpu.CompilerParams(
            collective_id=0, has_side_effects=True, vmem_limit_bytes=63_400_000
        ),
    )(table, rk, ru, rl[0, 0], rm[0, 0])
    return jnp.swapaxes(flag_grad, 2, 3), jnp.swapaxes(res_grad, 2, 3), helped[None]


def solution(mesh):
    tile_axes = ("groups", "sector", "pair")
    spec = lambda n: P("length", tile_axes, *([None] * n))
    return jax.shard_map(
        on_device,
        mesh=mesh,
        in_specs=(spec(3), spec(3), spec(2), spec(2), spec(1), spec(1), spec(3), spec(3), spec(2), spec(2)),
        out_specs=(spec(3), spec(3), spec(1)),
        check_vma=False,
    )
```
